256 devices in a mesh: sect: 2 (over x_hi), dev: 64 (over y, x_lo, z), cores: 2 (over core).
Axes of the slice: x: 4 (x_hi: 2, x_lo: 2; x = x_hi * 2 + x_lo), y: 4, z: 8, core: 2. Of those that a mesh axis runs over, the one named last changes fastest.
Arguments:
- query: bfloat16 [3072, 8192], P(('sect', 'dev'), 'cores'), may hold values from -30 to 30
- cache_keys: bfloat16 [3072, 128, 512], P(('sect', 'dev'), None, 'cores'), may hold values from -6 to 6
- cache_values: bfloat16 [3072, 128, 512], P(('sect', 'dev'), None, 'cores'), may hold values from -6 to 6
- new_key: bfloat16 [3072, 512], P(('sect', 'dev'), 'cores'), may hold values from -6 to 6
- new_value: bfloat16 [3072, 512], P(('sect', 'dev'), 'cores'), may hold values from -6 to 6
- lengths: int32 [3072], P(('sect', 'dev')), may hold values from 1 to 128
- hidden: bfloat16 [3072, 4096], P(('sect', 'dev')), may hold values from -6 to 6
- routes: int32 [3072, 8], P(('sect', 'dev')), may hold values from 0 to 63, all different within a row; in each aligned block of 24 rows (0 to 23, 24 to 47, ...) at most 6 rows name the same one
- gate_weights: float32 [3072, 8], P(('sect', 'dev')), may hold values from 0.1 to 1
- w_gate: bfloat16 [64, 4096, 1536], P('dev', None, ('sect', 'cores')), may hold values from -0.09375 to 0.09375
- w_up: bfloat16 [64, 4096, 1536], P('dev', None, ('sect', 'cores')), may hold values from -0.09375 to 0.09375
- w_down: bfloat16 [64, 4096, 1536], P('dev', None, ('sect', 'cores')), may hold values from -0.15625 to 0.15625
Outputs:
- attended: bfloat16 [3072, 8192], P(('sect', 'dev'), 'cores')
- expert_out: bfloat16 [3072, 4096], P(('sect', 'dev'), 'cores')
The draws below stay inside these ranges and needn't reach their ends.
Inputs may be any that keep to these rules, and one draw needn't show every extreme that they name: Each row names 8 different experts; the rows of one aligned block of 24 send at most 6 routes to one expert.
All inputs are finite; a program needn't handle non-finite values.
Results may differ from the reference program's by a relative error of at most 0.0075.
Values may be sent and summed in bfloat16 or wider, within the bound.
A program may use at most 128 MiB of HBM per device.

```python
import math
import jax
import jax.numpy as jnp
import numpy as np
from jax import lax

D = 4096
FF = 1536
HQ = 64
KVH = 4
HD = 128
TOPK = 8
R_DEV = 24
CACHE = 128
EXPERTS = 64
ROWS = 3072
CAP = 6


def draw_query(key, part):
    key = jax.random.fold_in(key, 11)
    return jax.random.truncated_normal(key, -6.0, 6.0, (ROWS, HQ * HD)).astype(jnp.bfloat16)


def draw_cache_keys(key, part):
    key = jax.random.fold_in(key, 12)
    return jax.random.truncated_normal(key, -6.0, 6.0, (ROWS, CACHE, KVH * HD)).astype(jnp.bfloat16)


def draw_lengths(key, part):
    key = jax.random.fold_in(key, 13)
    first, second = jax.random.split(key)
    drawn = jax.random.randint(first, (ROWS,), 1, CACHE + 1)
    rows = jnp.arange(ROWS)
    drawn = jnp.where(rows % R_DEV == 0, jnp.maximum(drawn, 2), drawn)
    drawn = jnp.where(rows == 1, 1, drawn)
    full = jax.random.randint(second, (), 0, ROWS // R_DEV) * R_DEV
    return jnp.where(rows == full, CACHE, drawn).astype(jnp.int32)


def steps_of(key, dims, cuts, low, high):
    def one(axis_at, blocks):
        heights = jax.random.uniform(jax.random.fold_in(jax.random.fold_in(key, 6), axis_at), (blocks,), jnp.float32, low / len(cuts), high / len(cuts))
        return jnp.repeat(jnp.exp(heights), dims[axis_at] // blocks).reshape((-1,) + (1,) * (len(dims) - axis_at - 1))

    factor_of = one(*cuts[0])
    for cut in cuts[1:]:
        factor_of = factor_of * one(*cut)
    return factor_of


def deal_out(key, own, number, rows, count, top, bound, skew):
    sequence = jax.random.permutation(key, count)
    heavy_load, usual = portions_of(count, rows * top, bound, skew, True), portions_of(count, rows * top, bound, skew, False)
    places = jnp.arange(count)

    def named(sizes, rotation):
        used = int((sizes > 0).sum())
        fixed = max(1, used // 4)
        moved = fixed + (places - fixed + rotation * (used - fixed)) % max(1, count - fixed)
        return jnp.zeros((count,), jnp.int32).at[sequence[jnp.where(places < fixed, places, moved)]].set(jnp.asarray(sizes, jnp.int32))

    sizes = jnp.where(number % 4 == 0, named(heavy_load, number // 4), named(usual, number - number // 4 - 1))
    mixed = jax.random.permutation(jax.random.fold_in(own, 3), count)
    donor, receiver = mixed[0:count // 2 * 2:2], mixed[1:count // 2 * 2:2]
    slack = jnp.minimum(sizes[donor] - 1, bound - sizes[receiver]) // 2
    slack = jnp.where((donor == sequence[0]) | (receiver == sequence[0]) | (sizes[receiver] == 0), 0, jnp.maximum(slack, 0))
    moved = jax.random.randint(jax.random.fold_in(own, 4), (count // 2,), 0, 1 << 20) % (slack + 1)
    sizes = sizes.at[donor].add(-moved).at[receiver].add(moved)
    members = jnp.searchsorted(jnp.cumsum(sizes), jnp.arange(rows * top), side="right").astype(jnp.int32)
    table = members.reshape(top, rows).T
    table = table[jax.random.permutation(jax.random.fold_in(own, 1), rows)]
    rotation = jax.random.randint(jax.random.fold_in(own, 2), (rows, 1), 0, top)
    return jnp.take_along_axis(table, (jnp.arange(top)[None, :] + rotation) % top, axis=1)


def portions_of(amount, total, reach, skew, full):
    weights = [(1 << 20) // math.isqrt(rank ** skew) + 1 for rank in range(1, amount + 1)]
    largest = reach if full else min(reach, max(-(-total // amount), total * weights[0] // sum(weights)))
    least = 1 if total - largest >= amount - 1 else 0
    counts, surplus = [largest] + [least] * (amount - 1), total - largest - least * (amount - 1)
    while surplus > 0:
        free = [i for i in range(1, amount) if counts[i] < largest] or [i for i in range(1, amount) if counts[i] < reach]
        whole, budget = sum([weights[i] for i in free]), surplus
        for i in free:
            extra = min(reach - counts[i], max(1, budget * weights[i] // whole), surplus)
            counts[i] = counts[i] + extra
            surplus = surplus - extra
    return np.array(counts)


def centred(rng, extent, deviation, reach, shards=(), held_as=jnp.bfloat16):
    loudness = steps_of(rng, extent, shards, -0.22, 0.18) if shards else 1.0
    values = jax.random.normal(rng, extent, jnp.float32) * deviation * loudness
    return jnp.minimum(jnp.maximum(values, -reach), reach).astype(held_as)


def setup_inputs(seed: int = 0) -> dict:
    streams_of = jax.random.split(jax.random.key(seed), 13)
    query = draw_query(jax.random.fold_in(streams_of[12], 71), 0)
    cache_keys = draw_cache_keys(jax.random.fold_in(streams_of[12], 71), 0)
    cache_values = centred(streams_of[2], (ROWS, CACHE, KVH * HD), 1.0, 6.0, ((0, 128), (2, 2)))
    new_key = centred(streams_of[3], (ROWS, KVH * HD), 1.0, 6.0, ((0, 128), (1, 2)))
    new_value = centred(streams_of[4], (ROWS, KVH * HD), 1.0, 6.0, ((0, 128), (1, 2)))
    lengths = draw_lengths(jax.random.fold_in(streams_of[12], 71), 0)
    hidden = centred(streams_of[6], (ROWS, D), 1.0, 6.0, ((0, 128),))
    routes_keys = jax.random.split(jax.random.fold_in(streams_of[7], 1), ROWS // R_DEV)
    routes_turns = jax.random.permutation(jax.random.fold_in(streams_of[7], 3), ROWS // R_DEV)
    routes = jax.vmap(lambda own, number: deal_out(jax.random.fold_in(streams_of[7], 2), own, number, R_DEV, EXPERTS, TOPK, CAP, 2))(routes_keys, routes_turns).reshape((ROWS, TOPK))
    gate_weights = jnp.clip(jnp.exp(math.log(1.0) - 2.3025851 * jax.random.uniform(streams_of[8], (ROWS, TOPK), jnp.float32) ** steps_of(streams_of[8], (ROWS, TOPK), ((0, 128),), -0.2, 0.2)), 0.1, 1.0)
    w_gate = centred(streams_of[9], (EXPERTS, D, FF), D ** -0.5, 0.09375, ((0, 64), (2, 4)))
    w_up = centred(streams_of[10], (EXPERTS, D, FF), D ** -0.5, 0.09375, ((0, 64), (2, 4)))
    w_down = centred(streams_of[11], (EXPERTS, D, FF), FF ** -0.5, 0.15625, ((0, 64), (2, 4)))
    return dict(query=query, cache_keys=cache_keys, cache_values=cache_values, new_key=new_key, new_value=new_value, lengths=lengths, hidden=hidden, routes=routes, gate_weights=gate_weights, w_gate=w_gate, w_up=w_up, w_down=w_down)


def block_slots(routes, experts, capacity):
    rows, topk = routes.shape
    flat = routes.reshape(rows * topk)
    onehot = (flat[:, None] == jnp.arange(experts, dtype=jnp.int32)[None, :]).astype(jnp.int32)
    before = jnp.cumsum(onehot, axis=0) - onehot
    slot = jnp.sum(before * onehot, axis=1)
    return (flat * capacity + slot).reshape(rows, topk).astype(jnp.int32)


def reference(query, cache_keys, cache_values, new_key, new_value, lengths, hidden, routes, gate_weights, w_gate, w_up, w_down):
    group = HQ // KVH
    scale = HD ** -0.5
    q_heads = query.astype(jnp.float32).reshape(ROWS, KVH, group, HD)
    keys = cache_keys.astype(jnp.float32).reshape(ROWS, CACHE, KVH, HD)
    values = cache_values.astype(jnp.float32).reshape(ROWS, CACHE, KVH, HD)
    scores = jnp.einsum("rkgd,rlkd->rkgl", q_heads, keys) * scale
    valid = jnp.arange(CACHE, dtype=jnp.int32)[None, :] < lengths[:, None]
    scores = jnp.where(valid[:, None, None, :], scores, -jnp.inf)
    own = jnp.einsum("rkgd,rkd->rkg", q_heads, new_key.astype(jnp.float32).reshape(ROWS, KVH, HD)) * scale
    top = jnp.maximum(jnp.max(scores, axis=-1), own)
    probs = jnp.exp(scores - top[..., None])
    own_p = jnp.exp(own - top)
    total = jnp.sum(probs, axis=-1) + own_p
    probs_b = (probs / total[..., None]).astype(jnp.bfloat16).astype(jnp.float32)
    own_b = (own_p / total).astype(jnp.bfloat16).astype(jnp.float32)
    mixed = jnp.einsum("rkgl,rlkd->rkgd", probs_b, values)
    mixed = mixed + own_b[..., None] * new_value.astype(jnp.float32).reshape(ROWS, KVH, 1, HD)
    attended = mixed.astype(jnp.bfloat16).reshape(ROWS, HQ * HD)

    blocks = ROWS // R_DEV
    places = jax.vmap(lambda block: block_slots(block, EXPERTS, CAP))(routes.reshape(blocks, R_DEV, TOPK))
    expert_id = (places // CAP).reshape(-1)
    slot = (places % CAP)
    position = (slot + (jnp.arange(blocks, dtype=jnp.int32) * CAP)[:, None, None]).reshape(-1)
    row_id = jnp.repeat(jnp.arange(ROWS, dtype=jnp.int32), TOPK)
    table = jnp.full((EXPERTS, blocks * CAP), ROWS, dtype=jnp.int32).at[expert_id, position].set(row_id)
    weights = jnp.zeros((EXPERTS, blocks * CAP), dtype=jnp.float32).at[expert_id, position].set(gate_weights.reshape(-1))
    padded = jnp.concatenate([hidden, jnp.zeros((1, D), dtype=hidden.dtype)], axis=0)

    def step(total, inputs):
        rows_of, weight_of, gate_w, up_w, down_w = inputs
        chosen = padded[rows_of]
        gate = jnp.dot(chosen, gate_w, preferred_element_type=jnp.float32)
        up = jnp.dot(chosen, up_w, preferred_element_type=jnp.float32)
        act = (jax.nn.silu(gate) * up).astype(jnp.bfloat16)
        result = lax.dot_general(act, down_w, (((1,), (1,)), ((), ())), preferred_element_type=jnp.float32)
        result = result.astype(jnp.bfloat16).astype(jnp.float32)
        total = total.at[rows_of].add(result * weight_of[:, None], mode="drop")
        return total, None

    start = jnp.zeros((ROWS, D), dtype=jnp.float32)
    total, unused = lax.scan(step, start, (table, weights, w_gate, w_up, w_down))
    return attended, total.astype(jnp.bfloat16)
```

```python
import functools

import jax
import jax.numpy as jnp
from jax import lax
from jax.experimental import pallas as pl
from jax.experimental.pallas import tpu as pltpu
from jax.sharding import PartitionSpec as P

MESH = pl.DeviceIdType.MESH
HD = 128
NX, NY, NZ = 4, 4, 8
R = 24
RP = 32
CAP = 6
S = NZ * CAP
W = 256
F32 = jnp.float32
BF16 = jnp.bfloat16


def dot(a, b):
    return jnp.dot(a, b, preferred_element_type=F32)


def dot_nt(a, b):
    return lax.dot_general(a, b, (((1,), (1,)), ((), ())), preferred_element_type=F32)


def wait_bytes(ref, sem):
    pltpu.make_async_copy(ref, ref, sem).wait()


def body(
    nc,
    hid, routes, gates, lens, query, new_k, new_v, keys_h, vals_h, wg_h, wu_h, wd_h,
    att_out, out,
    zb, cb, ct, pick, wtab, whl, ps, ob, xf, xo, gacc, uacc, act,
    so, ro, sx, rx, sy, ry, sz, rz, wg, wu, wd, keys, vals, qs, os, nk, nv,
    send, recv, loc,
):
    half = nc * W
    sect = lax.axis_index("sect")
    dev = lax.axis_index("dev")
    core = lax.axis_index("cores")
    xlo = lax.rem(dev // NZ, 2)
    x = sect * 2 + xlo
    y = dev // (2 * NZ)
    z = lax.rem(dev, NZ)

    def at(dx=0, dy=0, dz=0, dc=0):
        px = lax.rem(x + dx, NX)
        py = lax.rem(y + dy, NY)
        pz = lax.rem(z + dz, NZ)
        pc = lax.rem(core + dc, 2)
        return (px // 2, (py * 2 + lax.rem(px, 2)) * NZ + pz, pc)

    def push(src, dst, stage, c, to):
        pltpu.make_async_remote_copy(
            src_ref=src, dst_ref=dst, send_sem=send.at[stage, c], recv_sem=recv.at[stage, c],
            device_id=to, device_id_type=MESH,
        ).start()

    loads = [
        pltpu.make_async_copy(a, b, loc.at[i])
        for i, (a, b) in enumerate(
            ((keys_h, keys), (vals_h, vals), (wg_h, wg), (wu_h, wu), (wd_h, wd))
        )
    ]
    for load in loads:
        load.start()

    peers = (
        [at(dz=k) for k in range(1, NZ)]
        + [at(dy=k) for k in range(1, NY)]
        + [at(dx=k) for k in range(1, NX)]
        + [at(dc=1)]
    )
    barrier = pltpu.get_barrier_semaphore()
    for peer in peers:
        pl.semaphore_signal(barrier, inc=1, device_id=peer, device_id_type=MESH)

    lane = lax.broadcasted_iota(jnp.int32, (R, 128), 1)
    named = jnp.zeros((R, 128), F32)
    weight = jnp.zeros((R, 128), F32)
    for k in range(routes.shape[1]):
        route = routes[:, k : k + 1]
        named = named + jnp.where(lane == route, 1.0, 0.0)
        weight = weight + jnp.where(lane == route + 64, gates[:, k : k + 1], 0.0)
    row_i = lax.broadcasted_iota(jnp.int32, (R, R), 0)
    col_i = lax.broadcasted_iota(jnp.int32, (R, R), 1)
    earlier = dot(jnp.where(col_i < row_i, 1.0, 0.0).astype(BF16), named.astype(BF16))
    code = jnp.where(lane < 64, jnp.where(named > 0.5, earlier, -1.0), weight)
    lane_p = lax.broadcasted_iota(jnp.int32, (RP - R, 128), 1)
    cb[0] = jnp.concatenate([code, jnp.where(lane_p < 64, -1.0, 0.0)], axis=0)

    def stage_rows(c, _):
        cols = pl.ds(pl.multiple_of(core * half + c * W, W), W)
        rows = hid[:, cols].astype(F32)
        zb[c, 0] = jnp.concatenate([rows, jnp.zeros((RP - R, W), F32)], axis=0).astype(BF16)
        return 0

    lax.fori_loop(0, nc, stage_rows, 0)

    pl.semaphore_wait(barrier, len(peers))

    z_order = (4, 1, 7, 2, 6, 3, 5)
    for k in z_order:
        push(cb.at[0], cb.at[NZ - k], 8, 0, at(dz=k))

    def send_z(c, _):
        for k in z_order:
            push(zb.at[c, 0], zb.at[c, NZ - k], 0, c, at(dz=k))
        return 0

    lax.fori_loop(0, nc, send_z, 0)

    nk[...] = new_k[...].astype(F32)
    nv[...] = new_v[...].astype(F32)
    heads = query.shape[1] // HD
    for h in range(heads):
        qs[:, h, :] = query[:, h * HD : (h + 1) * HD].astype(F32)

    wait_bytes(cb.at[pl.ds(1, NZ - 1)], recv.at[8, 0])
    ct[...] = cb[...].reshape(NZ * RP, 128).T
    slot_i = lax.broadcasted_iota(jnp.int32, (S, NZ * RP), 0)
    slot_b = slot_i // CAP
    slot_s = (slot_i - slot_b * CAP).astype(F32)
    here = slot_b == lax.broadcasted_iota(jnp.int32, (S, NZ * RP), 1) // RP
    for d in range(NY):
        for q in range(2):
            expert = (lax.rem(y + d, NY) * 2 + lax.rem(xlo + q, 2)) * NZ + z
            mask = here & (ct[pl.ds(expert, 1), :] == slot_s)
            at_row = (d * 2 + q) * S
            pick[at_row : at_row + S, :] = jnp.where(mask, 1.0, 0.0).astype(BF16)
            wtab[at_row : at_row + S, :] = jnp.where(mask, ct[pl.ds(expert + 64, 1), :], 0.0)
    weights = wtab[...].T
    high = weights.astype(BF16)
    whl[0] = high
    whl[1] = (weights - high.astype(F32)).astype(BF16)

    gacc[...] = jnp.zeros_like(gacc)
    uacc[...] = jnp.zeros_like(uacc)

    scale = HD ** (-0.5)

    def attend(r):
        length = lens[r]
        q = qs[r]
        q0, q1 = q[: heads // 2], q[heads // 2 :]
        empty = jnp.zeros_like(q0)
        wide = jnp.concatenate(
            [jnp.concatenate([q0, empty], axis=1), jnp.concatenate([empty, q1], axis=1)], axis=0
        ).astype(BF16)
        scores = dot_nt(wide, keys[r]) * scale
        valid = lax.broadcasted_iota(jnp.int32, scores.shape, 1) < length
        scores = jnp.where(valid, scores, -jnp.inf)
        fresh_k = nk[pl.ds(r, 1), :]
        fresh_v = nv[pl.ds(r, 1), :]
        own = jnp.concatenate(
            [
                jnp.sum(q0 * fresh_k[:, :HD], axis=1, keepdims=True),
                jnp.sum(q1 * fresh_k[:, HD:], axis=1, keepdims=True),
            ],
            axis=0,
        ) * scale
        top = jnp.maximum(jnp.max(scores, axis=1, keepdims=True), own)
        probs = jnp.exp(scores - top)
        own_p = jnp.exp(own - top)
        total = jnp.sum(probs, axis=1, keepdims=True) + own_p
        probs_b = (probs / total).astype(BF16)
        own_b = (own_p / total).astype(BF16).astype(F32)
        mixed = dot(probs_b, vals[r])
        n = heads // 2
        os[r, :n] = mixed[:n, :HD] + own_b[:n] * fresh_v[:, :HD]
        os[r, n:] = mixed[n:, HD:] + own_b[n:] * fresh_v[:, HD:]

    per_step = R // nc
    half_rows = NX * NY * S // 2

    def gate_up(x_ref, c, base):
        depth = pl.ds(pl.multiple_of(base + c * W, W), W)

        def part(i, _):
            rows = pl.ds(pl.multiple_of(i * half_rows, half_rows), half_rows)
            block = x_ref[c, pl.ds(i * 2, 2)].reshape(half_rows, W)
            gacc[rows, :] += dot(block, wg[depth, :])
            uacc[rows, :] += dot(block, wu[depth, :])
            return 0

        lax.fori_loop(0, 2, part, 0)

    def forward(t, _):
        @pl.when(t < nc)
        def _():
            c = t
            wait_bytes(zb.at[c, pl.ds(1, NZ - 1)], recv.at[0, c])
            chosen = dot(pick[...], zb[c].reshape(NZ * RP, W)).astype(BF16)
            chosen = chosen.reshape(NY, 2, S, W)
            for d in range(1, NY):
                ps[c, d - 1] = chosen[d]
                push(ps.at[c, d - 1, 0], xf.at[c, 0, NY - d], 1, c, at(dy=d))
                push(ps.at[c, d - 1, 1], ob.at[c, NY - d], 2, c, at(dy=d))
            xf[c, 0, 0] = chosen[0, 0]
            ob[c, 0] = chosen[0, 1]

        @pl.when((t >= 1) & (t < nc + 1))
        def _():
            c = t - 1
            wait_bytes(xf.at[c, 0, pl.ds(1, NY - 1)], recv.at[1, c])
            wait_bytes(ob.at[c, pl.ds(1, NY - 1)], recv.at[2, c])
            push(xf.at[c, 0], xf.at[c, 2], 3, c, at(dx=2))
            push(ob.at[c], xf.at[c, 3], 3, c, at(dx=1))
            push(ob.at[c], xf.at[c, 1], 3, c, at(dx=3))

        @pl.when((t >= 2) & (t < nc + 2))
        def _():
            c = t - 2
            wait_bytes(xf.at[c, pl.ds(1, NX - 1)], recv.at[3, c])
            push(xf.at[c], xo.at[c], 4, c, at(dc=1))
            gate_up(xf, c, core * half)

        @pl.when(t >= 3)
        def _():
            c = t - 3
            wait_bytes(xo.at[c], recv.at[4, c])
            gate_up(xo, c, (1 - core) * half)

        @pl.when(t < nc)
        def _():
            for i in range(per_step):
                attend(t * per_step + i)

        return 0

    for load in loads[:4]:
        load.wait()
    lax.fori_loop(0, nc + 3, forward, 0)

    def activate(i, _):
        rows = pl.ds(pl.multiple_of(i * S, S), S)
        gate = gacc[rows, :]
        act[rows, :] = (gate * jax.nn.sigmoid(gate) * uacc[rows, :]).astype(BF16)
        return 0

    lax.fori_loop(0, NX * NY, activate, 0)
    loads[4].wait()

    def down(c, base, i):
        depth = pl.ds(pl.multiple_of(base + c * W, W), W)
        rows = pl.ds(pl.multiple_of(i * half_rows, half_rows), half_rows)
        return dot_nt(act[rows, :], wd[depth, :])

    def backward(t, _):
        @pl.when(t < nc)
        def _():
            c = t

            def part(i, _):
                got = down(c, (1 - core) * half, i)
                so[c, pl.ds(i * 2, 2)] = got.astype(BF16).reshape(2, NY, S, W)
                return 0

            lax.fori_loop(0, 2, part, 0)
            push(so.at[c], ro.at[c], 5, c, at(dc=1))

        @pl.when((t >= 1) & (t < nc + 1))
        def _():
            c = t - 1
            wait_bytes(ro.at[c], recv.at[5, c])

            def part(i, _):
                got = down(c, core * half, i) + ro[c, pl.ds(i * 2, 2)].reshape(
                    half_rows, W
                ).astype(F32)
                sx[c, pl.ds(i * 2, 2)] = got.astype(BF16).reshape(2, NY, S, W)
                return 0

            lax.fori_loop(0, 2, part, 0)
            push(sx.at[c, 2], rx.at[c, 2], 6, c, at(dx=2))
            push(sx.at[c, 1], rx.at[c, 0], 6, c, at(dx=1))
            push(sx.at[c, 3], rx.at[c, 1], 6, c, at(dx=3))

        @pl.when((t >= 2) & (t < nc + 2))
        def _():
            c = t - 2
            wait_bytes(rx.at[c], recv.at[6, c])
            for j in range(NY):
                mine = (sx[c, 0, j].astype(F32) + rx[c, 2, j].astype(F32)).astype(BF16)
                other = (rx[c, 0, j].astype(F32) + rx[c, 1, j].astype(F32)).astype(BF16)
                if j == 0:
                    ry[c, 0, 0] = mine
                    ry[c, 0, 1] = other
                else:
                    sy[c, j - 1, 0] = mine
                    sy[c, j - 1, 1] = other
                    push(sy.at[c, j - 1], ry.at[c, NY - j], 7, c, at(dy=j))

        @pl.when((t >= 3) & (t < nc + 3))
        def _():
            c = t - 3
            wait_bytes(ry.at[c, pl.ds(1, NY - 1)], recv.at[7, c])
            slots = ry[c].reshape(NY * 2 * S, W)
            sums = dot(whl[0], slots) + dot(whl[1], slots)
            sz[c] = sums.astype(BF16).reshape(NZ, RP, W)
            for k in z_order:
                push(sz.at[c, k], rz.at[c, NZ - k - 1], 9, c, at(dz=k))

        @pl.when(t >= 4)
        def _():
            c = t - 4
            wait_bytes(rz.at[c], recv.at[9, c])
            total = sz[c, 0].astype(F32)
            for k in range(NZ - 1):
                total = total + rz[c, k].astype(F32)
            cols = pl.ds(pl.multiple_of(c * W, W), W)
            out[:, cols] = total[:R].astype(BF16)

        return 0

    lax.fori_loop(0, nc + 4, backward, 0)

    for h in range(heads):
        att_out[:, h * HD : (h + 1) * HD] = os[:, h, :].astype(BF16)

    def drain(c, _):
        wait_bytes(zb.at[c, pl.ds(1, NZ - 1)], send.at[0, c])
        wait_bytes(xf.at[c, 0, pl.ds(1, NY - 1)], send.at[1, c])
        wait_bytes(ob.at[c, pl.ds(1, NY - 1)], send.at[2, c])
        wait_bytes(xf.at[c, pl.ds(1, NX - 1)], send.at[3, c])
        wait_bytes(xo.at[c], send.at[4, c])
        wait_bytes(ro.at[c], send.at[5, c])
        wait_bytes(rx.at[c], send.at[6, c])
        wait_bytes(ry.at[c, pl.ds(1, NY - 1)], send.at[7, c])
        wait_bytes(rz.at[c], send.at[9, c])
        return 0

    wait_bytes(cb.at[pl.ds(1, NZ - 1)], send.at[8, 0])
    lax.fori_loop(0, nc, drain, 0)


def per_device(
    query, cache_keys, cache_values, new_key, new_value, lengths,
    hidden, routes, gate_weights, w_gate, w_up, w_down,
):
    width = hidden.shape[1]
    nc = width // 2 // W
    inner = w_gate.shape[2]
    rows = NX * NY * S
    heads = query.shape[1] // HD
    vmem = pl.BlockSpec(memory_space=pltpu.VMEM)
    smem = pl.BlockSpec(memory_space=pltpu.SMEM)
    hbm = pl.BlockSpec(memory_space=pl.ANY)
    shapes = [
        ((nc, NZ, RP, W), BF16),
        ((NZ, RP, 128), F32),
        ((128, NZ * RP), F32),
        ((NY * 2 * S, NZ * RP), BF16),
        ((NY * 2 * S, NZ * RP), F32),
        ((2, NZ * RP, NY * 2 * S), BF16),
        ((nc, NY - 1, 2, S, W), BF16),
        ((nc, NY, S, W), BF16),
        ((nc, NX, NY, S, W), BF16),
        ((nc, NX, NY, S, W), BF16),
        ((rows, inner), F32),
        ((rows, inner), F32),
        ((rows, inner), BF16),
        ((nc, NX, NY, S, W), BF16),
        ((nc, NX, NY, S, W), BF16),
        ((nc, NX, NY, S, W), BF16),
        ((nc, NX - 1, NY, S, W), BF16),
        ((nc, NY - 1, 2, S, W), BF16),
        ((nc, NY, 2, S, W), BF16),
        ((nc, NZ, RP, W), BF16),
        ((nc, NZ - 1, RP, W), BF16),
        ((width, inner), BF16),
        ((width, inner), BF16),
        ((width, inner), BF16),
        (cache_keys.shape, BF16),
        (cache_values.shape, BF16),
        ((R, heads, HD), F32),
        ((R, heads, HD), F32),
        (new_key.shape, F32),
        (new_value.shape, F32),
    ]
    return pl.pallas_call(
        functools.partial(body, nc),
        out_shape=(
            jax.ShapeDtypeStruct(query.shape, BF16),
            jax.ShapeDtypeStruct((R, width // 2), BF16),
        ),
        in_specs=[vmem, vmem, vmem, smem, vmem, vmem, vmem, hbm, hbm, hbm, hbm, hbm],
        out_specs=(vmem, vmem),
        scratch_shapes=[pltpu.VMEM(s, t) for s, t in shapes]
        + [
            pltpu.SemaphoreType.DMA((10, nc)),
            pltpu.SemaphoreType.DMA((10, nc)),
            pltpu.SemaphoreType.DMA((5,)),
        ],
        compiler_params=pltpu.CompilerParams(
            collective_id=0, has_side_effects=True, vmem_limit_bytes=60 * 1024 * 1024
        ),
        name="experts",
    )(
        hidden, routes, gate_weights, lengths, query, new_key, new_value,
        cache_keys, cache_values, w_gate[0], w_up[0], w_down[0],
    )


def solution(mesh):
    rows = ("sect", "dev")
    cols = ("sect", "cores")
    in_specs = (
        P(rows, "cores"),
        P(rows, None, "cores"),
        P(rows, None, "cores"),
        P(rows, "cores"),
        P(rows, "cores"),
        P(rows),
        P(rows, None),
        P(rows, None),
        P(rows, None),
        P("dev", None, cols),
        P("dev", None, cols),
        P("dev", None, cols),
    )
    out_specs = (P(rows, "cores"), P(rows, "cores"))
    return jax.shard_map(
        per_device, mesh=mesh, in_specs=in_specs, out_specs=out_specs, check_vma=False
    )
```

```python
import functools

import jax
import jax.numpy as jnp
from jax import lax
from jax.experimental import pallas as pl
from jax.experimental.pallas import tpu as pltpu
from jax.sharding import PartitionSpec as P

MESH = pl.DeviceIdType.MESH
HD = 128
NX, NY, NZ = 4, 4, 8
R = 24
RP = 32
CAP = 6
ZR = NZ * 2 * R
S = NZ * CAP
W = 256
F_LAGS = (2, 4, 7, 9, 10)
B_LAGS = (1, 3, 5, 7, 9, 11)
F32 = jnp.float32
BF16 = jnp.bfloat16


def dot(a, b):
    return jnp.dot(a, b, preferred_element_type=F32)


def dot_nt(a, b):
    return lax.dot_general(a, b, (((1,), (1,)), ((), ())), preferred_element_type=F32)


def wait_bytes(ref, sem):
    pltpu.make_async_copy(ref, ref, sem).wait()


def body(
    nc,
    hid, routes_t, gates_t, lens, query, new_k, new_v, keys_h, vals_h, wg_h, wu_h, wd_h,
    att_out, out,
    hs, hp, zb, cb, ct, pick, wtab, whl, ps, ob, xf, xo, gacc, uacc, act,
    so, ro, sx, rx, sy, ry, sz, r1, s2, r2, fo, fs, fr, wg, wu, wd, keys, vals, qs, os, nk, nv,
    send, recv, loc,
):
    half = nc * W
    sect = lax.axis_index("sect")
    dev = lax.axis_index("dev")
    core = lax.axis_index("cores")
    xlo = lax.rem(dev // NZ, 2)
    x = sect * 2 + xlo
    y = dev // (2 * NZ)
    z = lax.rem(dev, NZ)

    def at(dx=0, dy=0, dz=0, dc=0):
        px = lax.rem(x + dx, NX)
        py = lax.rem(y + dy, NY)
        pz = lax.rem(z + dz, NZ)
        pc = lax.rem(core + dc, 2)
        return (px // 2, (py * 2 + lax.rem(px, 2)) * NZ + pz, pc)

    def push(src, dst, stage, c, to):
        pltpu.make_async_remote_copy(
            src_ref=src, dst_ref=dst, send_sem=send.at[stage, c], recv_sem=recv.at[stage, c],
            device_id=to, device_id_type=MESH,
        ).start()

    loads = [
        pltpu.make_async_copy(a, b, loc.at[i])
        for i, (a, b) in enumerate(
            ((keys_h, keys), (vals_h, vals), (wg_h, wg), (wu_h, wu), (wd_h, wd))
        )
    ]
    for load in loads:
        load.start()

    peers = (
        [at(dz=k) for k in range(1, NZ)]
        + [at(dy=k) for k in range(1, NY)]
        + [at(dx=k) for k in range(1, NX)]
        + [at(dc=1)]
    )
    barrier = pltpu.get_barrier_semaphore()
    for peer in peers:
        pl.semaphore_signal(barrier, inc=1, device_id=peer, device_id_type=MESH)

    row_i = lax.broadcasted_iota(jnp.int32, (R, R), 0)
    col_i = lax.broadcasted_iota(jnp.int32, (R, R), 1)
    same = jnp.where(row_i == col_i, 1.0, 0.0)

    def turned(v):
        return lax.dot_general(
            same, v, (((1,), (1,)), ((), ())),
            precision=lax.Precision.HIGHEST, preferred_element_type=F32,
        )

    routes = turned(routes_t[...].astype(F32))
    gates = turned(gates_t[...])
    lane = lax.broadcasted_iota(jnp.int32, (R, 128), 1)
    lane_f = lane.astype(F32)
    named = jnp.zeros((R, 128), F32)
    weight = jnp.zeros((R, 128), F32)
    for k in range(routes.shape[1]):
        route = routes[:, k : k + 1]
        named = named + jnp.where(lane_f == route, 1.0, 0.0)
        weight = weight + jnp.where(lane_f == route + 64.0, gates[:, k : k + 1], 0.0)
    earlier = dot(jnp.where(col_i < row_i, 1.0, 0.0).astype(BF16), named.astype(BF16))
    cb[0, :R] = jnp.where(lane < 64, jnp.where(named > 0.5, earlier, -1.0), weight)

    def own_rows(c):
        cols = pl.ds(pl.multiple_of(core * half + c * W, W), W)
        return hid[:, cols].astype(F32)

    def stage_rows(c, _):
        hs[c] = jnp.concatenate([own_rows(c), jnp.zeros((RP - R, W), F32)], axis=0).astype(BF16)
        return 0

    lax.fori_loop(0, nc, stage_rows, 0)

    pl.semaphore_wait(barrier, len(peers))

    def send_rows(c, _):
        push(hs.at[c], hp.at[c], 0, c, at(dx=2))
        return 0

    push(hs.at[0], hp.at[0], 0, 0, at(dx=2))
    push(cb.at[0, pl.ds(0, R)], cb.at[0, pl.ds(R, R)], 7, 0, at(dx=2))
    lax.fori_loop(1, nc, send_rows, 0)

    nk[...] = new_k[...].astype(F32)
    nv[...] = new_v[...].astype(F32)
    heads = query.shape[1] // HD
    for h in range(heads):
        qs[:, h, :] = query[:, h * HD : (h + 1) * HD].astype(F32)
    gacc[...] = jnp.zeros_like(gacc)
    uacc[...] = jnp.zeros_like(uacc)

    wait_bytes(cb.at[0, pl.ds(R, R)], recv.at[7, 0])

    def send_codes():
        for k in (4, 1, 7, 2, 6, 3, 5):
            push(cb.at[0], cb.at[NZ - k], 7, 1, at(dz=k))

    def tables():
        wait_bytes(cb.at[pl.ds(1, NZ - 1)], recv.at[7, 1])
        ct[...] = cb[...].reshape(ZR, 128).T
        slot_i = lax.broadcasted_iota(jnp.int32, (S, ZR), 0)
        slot_b = slot_i // CAP
        slot_s = (slot_i - slot_b * CAP).astype(F32)
        place = lax.broadcasted_iota(jnp.int32, (S, ZR), 1)
        place_b = place // (2 * R)
        partner = place - place_b * (2 * R) >= R
        here = slot_b == place_b
        for d in range(NY):
            for kind in range(3):
                q = kind // 2
                expert = (lax.rem(y + d, NY) * 2 + lax.rem(xlo + q, 2)) * NZ + z
                block = partner if kind == 1 else jnp.logical_not(partner)
                mask = here & block & (ct[pl.ds(expert, 1), :] == slot_s)
                at_row = (d * 3 + kind) * S
                pick[at_row : at_row + S, :] = jnp.where(mask, 1.0, 0.0).astype(BF16)
                wtab[at_row : at_row + S, :] = jnp.where(mask, ct[pl.ds(expert + 64, 1), :], 0.0)

    scale = HD ** (-0.5)

    def attend(r):
        length = lens[r]
        q = qs[r]
        q0, q1 = q[: heads // 2], q[heads // 2 :]
        empty = jnp.zeros_like(q0)
        wide = jnp.concatenate(
            [jnp.concatenate([q0, empty], axis=1), jnp.concatenate([empty, q1], axis=1)], axis=0
        ).astype(BF16)
        scores = dot_nt(wide, keys[r]) * scale
        valid = lax.broadcasted_iota(jnp.int32, scores.shape, 1) < length
        scores = jnp.where(valid, scores, -jnp.inf)
        fresh_k = nk[pl.ds(r, 1), :]
        fresh_v = nv[pl.ds(r, 1), :]
        own = jnp.concatenate(
            [
                jnp.sum(q0 * fresh_k[:, :HD], axis=1, keepdims=True),
                jnp.sum(q1 * fresh_k[:, HD:], axis=1, keepdims=True),
            ],
            axis=0,
        ) * scale
        top = jnp.maximum(jnp.max(scores, axis=1, keepdims=True), own)
        probs = jnp.exp(scores - top)
        own_p = jnp.exp(own - top)
        total = jnp.sum(probs, axis=1, keepdims=True) + own_p
        probs_b = (probs / total).astype(BF16)
        own_b = (own_p / total).astype(BF16).astype(F32)
        mixed = dot(probs_b, vals[r])
        n = heads // 2
        os[r, :n] = mixed[:n, :HD] + own_b[:n] * fresh_v[:, :HD]
        os[r, n:] = mixed[n:, HD:] + own_b[n:] * fresh_v[:, HD:]

    per_step = R // nc
    half_rows = NX * NY * S // 2

    def gate_up(x_ref, c, base):
        depth = pl.ds(pl.multiple_of(base + c * W, W), W)

        def part(i, _):
            rows = pl.ds(pl.multiple_of(i * half_rows, half_rows), half_rows)
            block = x_ref[c, pl.ds(i * 2, 2)].reshape(half_rows, W)
            gacc[rows, :] += dot(block, wg[depth, :])
            uacc[rows, :] += dot(block, wu[depth, :])
            return 0

        lax.fori_loop(0, 2, part, 0)

    def forward(t, _):
        @pl.when(t < nc)
        def _():
            c = t
            wait_bytes(hp.at[c], recv.at[0, c])
            zb[c, 0] = jnp.concatenate([own_rows(c), hp[c].astype(F32)[:R]], axis=0).astype(BF16)
            push(zb.at[c, 0], zb.at[c, 4], 1, c, at(dz=4))
            push(zb.at[c, 0], zb.at[c, 7], 1, c, at(dz=1))
            push(zb.at[c, 0], zb.at[c, 1], 1, c, at(dz=7))

        @pl.when(t == 0)
        def _():
            send_codes()

        @pl.when((t >= F_LAGS[0]) & (t < nc + F_LAGS[0]))
        def _():
            c = t - F_LAGS[0]
            wait_bytes(zb.at[c, pl.ds(1, 3)], recv.at[1, c])
            push(zb.at[c, 4], zb.at[c, 3], 2, c, at(dz=1))
            push(zb.at[c, 4], zb.at[c, 5], 2, c, at(dz=7))
            push(zb.at[c, 7], zb.at[c, 6], 2, c, at(dz=1))
            push(zb.at[c, 1], zb.at[c, 2], 2, c, at(dz=7))

        @pl.when(t == F_LAGS[1])
        def _():
            tables()

        @pl.when((t >= F_LAGS[1]) & (t < nc + F_LAGS[1]))
        def _():
            c = t - F_LAGS[1]
            wait_bytes(zb.at[c, pl.ds(1, 4)], recv.at[2, c])
            chosen = dot(pick[...], zb[c].reshape(ZR, W)).astype(BF16)
            chosen = chosen.reshape(NY, 3, S, W)
            for d in (2, 1, 3):
                ps[c, d - 1] = chosen[d]
                push(ps.at[c, d - 1, pl.ds(0, 2)], xf.at[c, pl.ds(0, 2), NY - d], 3, c, at(dy=d))
                push(ps.at[c, d - 1, 2], ob.at[c, NY - d], 4, c, at(dy=d))
            xf[c, 0, 0] = chosen[0, 0]
            xf[c, 1, 0] = chosen[0, 1]
            ob[c, 0] = chosen[0, 2]

        @pl.when((t >= F_LAGS[2]) & (t < nc + F_LAGS[2]))
        def _():
            c = t - F_LAGS[2]
            wait_bytes(ob.at[c, pl.ds(1, NY - 1)], recv.at[4, c])
            push(ob.at[c], xf.at[c, 3], 5, c, at(dx=1))
            push(ob.at[c], xf.at[c, 2], 5, c, at(dx=3))

        @pl.when((t >= F_LAGS[3]) & (t < nc + F_LAGS[3]))
        def _():
            c = t - F_LAGS[3]
            wait_bytes(xf.at[c, pl.ds(0, 2), pl.ds(1, NY - 1)], recv.at[3, c])
            wait_bytes(xf.at[c, pl.ds(2, 2)], recv.at[5, c])
            push(xf.at[c], xo.at[c], 6, c, at(dc=1))
            gate_up(xf, c, core * half)

        @pl.when((t >= F_LAGS[4]) & (t < nc + F_LAGS[4]))
        def _():
            c = t - F_LAGS[4]
            wait_bytes(xo.at[c], recv.at[6, c])
            gate_up(xo, c, (1 - core) * half)

        @pl.when(t < nc)
        def _():
            for i in range(per_step):
                attend(t * per_step + i)

        @pl.when(t == nc)
        def _():
            weights = wtab[...].T
            high = weights.astype(BF16)
            whl[0] = high
            whl[1] = (weights - high.astype(F32)).astype(BF16)

        return 0

    for load in loads[:4]:
        load.wait()
    lax.fori_loop(0, nc + F_LAGS[-1], forward, 0)

    def activate(i, _):
        rows = pl.ds(pl.multiple_of(i * S, S), S)
        gate = gacc[rows, :]
        act[rows, :] = (gate * jax.nn.sigmoid(gate) * uacc[rows, :]).astype(BF16)
        return 0

    lax.fori_loop(0, NX * NY, activate, 0)
    loads[4].wait()

    def down(c, base, i):
        depth = pl.ds(pl.multiple_of(base + c * W, W), W)
        rows = pl.ds(pl.multiple_of(i * half_rows, half_rows), half_rows)
        return dot_nt(act[rows, :], wd[depth, :])

    def plus(a, *others):
        total = a.astype(F32)
        for b in others:
            total = total + b.astype(F32)
        return total

    def backward(t, _):
        @pl.when(t < nc)
        def _():
            c = t

            def part(i, _):
                got = down(c, (1 - core) * half, i)
                so[c, pl.ds(i * 2, 2)] = got.astype(BF16).reshape(2, NY, S, W)
                return 0

            lax.fori_loop(0, 2, part, 0)
            push(so.at[c], ro.at[c], 8, c, at(dc=1))

        @pl.when((t >= B_LAGS[0]) & (t < nc + B_LAGS[0]))
        def _():
            c = t - B_LAGS[0]
            wait_bytes(ro.at[c], recv.at[8, c])

            def part(i, _):
                theirs = ro[c, pl.ds(i * 2, 2)].reshape(half_rows, W)
                got = down(c, core * half, i) + theirs.astype(F32)
                sx[c, pl.ds(i * 2, 2)] = got.astype(BF16).reshape(2, NY, S, W)
                return 0

            lax.fori_loop(0, 2, part, 0)
            push(sx.at[c, 2], rx.at[c, 0], 9, c, at(dx=1))
            push(sx.at[c, 3], rx.at[c, 1], 9, c, at(dx=3))
            for j in (2, 1, 3):
                push(sx.at[c, pl.ds(0, 2), j], ry.at[c, NY - j, pl.ds(0, 2)], 10, c, at(dy=j))
            ry[c, 0, 0] = sx[c, 0, 0]
            ry[c, 0, 1] = sx[c, 1, 0]

        @pl.when((t >= B_LAGS[1]) & (t < nc + B_LAGS[1]))
        def _():
            c = t - B_LAGS[1]
            wait_bytes(rx.at[c], recv.at[9, c])
            for j in (2, 1, 3):
                sy[c, j - 1] = plus(rx[c, 0, j], rx[c, 1, j]).astype(BF16)
                push(sy.at[c, j - 1], ry.at[c, NY - j, 2], 11, c, at(dy=j))
            ry[c, 0, 2] = plus(rx[c, 0, 0], rx[c, 1, 0]).astype(BF16)

        @pl.when((t >= B_LAGS[2]) & (t < nc + B_LAGS[2]))
        def _():
            c = t - B_LAGS[2]
            wait_bytes(ry.at[c, pl.ds(1, NY - 1), pl.ds(0, 2)], recv.at[10, c])
            wait_bytes(ry.at[c, pl.ds(1, NY - 1), 2], recv.at[11, c])
            slots = ry[c].reshape(NY * 3 * S, W)
            sums = dot(whl[0], slots) + dot(whl[1], slots)
            sz[c] = sums.astype(BF16).reshape(NZ, 2 * R, W)
            push(sz.at[c, 6], r1.at[c, 0], 12, c, at(dz=7))
            push(sz.at[c, 2], r1.at[c, 1], 12, c, at(dz=1))
            push(sz.at[c, 5], r1.at[c, 2], 12, c, at(dz=1))
            push(sz.at[c, 3], r1.at[c, 3], 12, c, at(dz=7))

        @pl.when((t >= B_LAGS[3]) & (t < nc + B_LAGS[3]))
        def _():
            c = t - B_LAGS[3]
            wait_bytes(r1.at[c], recv.at[12, c])
            s2[c, 2] = plus(sz[c, 4], r1[c, 2], r1[c, 3]).astype(BF16)
            push(s2.at[c, 2], r2.at[c, 2], 13, c, at(dz=4))
            s2[c, 0] = plus(sz[c, 7], r1[c, 0]).astype(BF16)
            push(s2.at[c, 0], r2.at[c, 0], 13, c, at(dz=7))
            s2[c, 1] = plus(sz[c, 1], r1[c, 1]).astype(BF16)
            push(s2.at[c, 1], r2.at[c, 1], 13, c, at(dz=1))

        @pl.when((t >= B_LAGS[4]) & (t < nc + B_LAGS[4]))
        def _():
            c = t - B_LAGS[4]
            wait_bytes(r2.at[c], recv.at[13, c])
            total = plus(sz[c, 0], r2[c, 0], r2[c, 1], r2[c, 2])
            fo[c] = total[:R]
            fs[c] = jnp.concatenate([total[R:], jnp.zeros((RP - R, W), F32)], axis=0).astype(BF16)
            push(fs.at[c], fr.at[c], 14, c, at(dx=2))

        @pl.when((t >= B_LAGS[5]) & (t < nc + B_LAGS[5]))
        def _():
            c = t - B_LAGS[5]
            wait_bytes(fr.at[c], recv.at[14, c])
            cols = pl.ds(pl.multiple_of(c * W, W), W)
            out[:, cols] = (fo[c] + fr[c].astype(F32)[:R]).astype(BF16)

        @pl.when(t == 2)
        def _():
            for h in range(heads):
                att_out[:, h * HD : (h + 1) * HD] = os[:, h, :].astype(BF16)

        return 0

    lax.fori_loop(0, nc + B_LAGS[-1], backward, 0)

    def drain(c, _):
        wait_bytes(hp.at[c], send.at[0, c])
        wait_bytes(zb.at[c, pl.ds(1, 3)], send.at[1, c])
        wait_bytes(zb.at[c, pl.ds(1, 4)], send.at[2, c])
        wait_bytes(xf.at[c, pl.ds(0, 2), pl.ds(1, NY - 1)], send.at[3, c])
        wait_bytes(ob.at[c, pl.ds(1, NY - 1)], send.at[4, c])
        wait_bytes(xf.at[c, pl.ds(2, 2)], send.at[5, c])
        wait_bytes(xo.at[c], send.at[6, c])
        wait_bytes(ro.at[c], send.at[8, c])
        wait_bytes(rx.at[c], send.at[9, c])
        wait_bytes(ry.at[c, pl.ds(1, NY - 1), pl.ds(0, 2)], send.at[10, c])
        wait_bytes(ry.at[c, pl.ds(1, NY - 1), 2], send.at[11, c])
        wait_bytes(r1.at[c], send.at[12, c])
        wait_bytes(r2.at[c], send.at[13, c])
        wait_bytes(fr.at[c], send.at[14, c])
        return 0

    wait_bytes(cb.at[0, pl.ds(R, R)], send.at[7, 0])
    wait_bytes(cb.at[pl.ds(1, NZ - 1)], send.at[7, 1])
    lax.fori_loop(0, nc, drain, 0)


def per_device(
    query, cache_keys, cache_values, new_key, new_value, lengths,
    hidden, routes, gate_weights, w_gate, w_up, w_down,
):
    width = hidden.shape[1]
    nc = width // 2 // W
    inner = w_gate.shape[2]
    rows = NX * NY * S
    heads = query.shape[1] // HD
    vmem = pl.BlockSpec(memory_space=pltpu.VMEM)
    smem = pl.BlockSpec(memory_space=pltpu.SMEM)
    hbm = pl.BlockSpec(memory_space=pl.ANY)
    shapes = [
        ((nc, RP, W), BF16),
        ((nc, RP, W), BF16),
        ((nc, NZ, 2 * R, W), BF16),
        ((NZ, 2 * R, 128), F32),
        ((128, ZR), F32),
        ((NY * 3 * S, ZR), BF16),
        ((NY * 3 * S, ZR), F32),
        ((2, ZR, NY * 3 * S), BF16),
        ((nc, NY - 1, 3, S, W), BF16),
        ((nc, NY, S, W), BF16),
        ((nc, NX, NY, S, W), BF16),
        ((nc, NX, NY, S, W), BF16),
        ((rows, inner), F32),
        ((rows, inner), F32),
        ((rows, inner), BF16),
        ((nc, NX, NY, S, W), BF16),
        ((nc, NX, NY, S, W), BF16),
        ((nc, NX, NY, S, W), BF16),
        ((nc, 2, NY, S, W), BF16),
        ((nc, NY - 1, S, W), BF16),
        ((nc, NY, 3, S, W), BF16),
        ((nc, NZ, 2 * R, W), BF16),
        ((nc, 4, 2 * R, W), BF16),
        ((nc, 3, 2 * R, W), BF16),
        ((nc, 3, 2 * R, W), BF16),
        ((nc, R, W), F32),
        ((nc, RP, W), BF16),
        ((nc, RP, W), BF16),
        ((width, inner), BF16),
        ((width, inner), BF16),
        ((width, inner), BF16),
        (cache_keys.shape, BF16),
        (cache_values.shape, BF16),
        ((R, heads, HD), F32),
        ((R, heads, HD), F32),
        (new_key.shape, F32),
        (new_value.shape, F32),
    ]
    return pl.pallas_call(
        functools.partial(body, nc),
        out_shape=(
            jax.ShapeDtypeStruct(query.shape, BF16),
            jax.ShapeDtypeStruct((R, width // 2), BF16),
        ),
        in_specs=[vmem, vmem, vmem, smem, vmem, vmem, vmem, hbm, hbm, hbm, hbm, hbm],
        out_specs=(vmem, vmem),
        scratch_shapes=[pltpu.VMEM(s, t) for s, t in shapes]
        + [
            pltpu.SemaphoreType.DMA((15, nc)),
            pltpu.SemaphoreType.DMA((15, nc)),
            pltpu.SemaphoreType.DMA((5,)),
        ],
        compiler_params=pltpu.CompilerParams(
            collective_id=0, has_side_effects=True, vmem_limit_bytes=60 * 1024 * 1024
        ),
        name="experts",
    )(
        hidden, routes.T, gate_weights.T, lengths, query, new_key, new_value,
        cache_keys, cache_values, w_gate[0], w_up[0], w_down[0],
    )


def solution(mesh):
    rows = ("sect", "dev")
    cols = ("sect", "cores")
    in_specs = (
        P(rows, "cores"),
        P(rows, None, "cores"),
        P(rows, None, "cores"),
        P(rows, "cores"),
        P(rows, "cores"),
        P(rows),
        P(rows, None),
        P(rows, None),
        P(rows, None),
        P("dev", None, cols),
        P("dev", None, cols),
        P("dev", None, cols),
    )
    out_specs = (P(rows, "cores"), P(rows, "cores"))
    return jax.shard_map(
        per_device, mesh=mesh, in_specs=in_specs, out_specs=out_specs, check_vma=False
    )
```

```python
import functools

import jax
import jax.numpy as jnp
from jax import lax
from jax.experimental import pallas as pl
from jax.experimental.pallas import tpu as pltpu
from jax.sharding import PartitionSpec as P

MESH = pl.DeviceIdType.MESH
HD = 128
NX, NY, NZ = 4, 4, 8
R = 24
RP = 32
CAP = 6
ZR = NZ * 2 * R
S = NZ * CAP
W = 256
F_LAGS = (2, 4, 7, 9, 10)
B_LAGS = (1, 3, 5, 7, 9, 11)
F32 = jnp.float32
BF16 = jnp.bfloat16


def dot(a, b):
    return jnp.dot(a, b, preferred_element_type=F32)


def dot_nt(a, b):
    return lax.dot_general(a, b, (((1,), (1,)), ((), ())), preferred_element_type=F32)


def wait_bytes(ref, sem):
    pltpu.make_async_copy(ref, ref, sem).wait()


def body(
    nc,
    hid, routes_t, gates_t, lens, query, new_k, new_v, keys_h, vals_h, wg_h, wu_h, wd_h,
    att_out, out,
    hs, hp, zb, cb, ct, pick, wtab, whl, ps, ob, xf, xo, gacc, uacc, act,
    so, ro, sx, rx, sy, ry, sz, r1, s2, r2, fo, fs, fr, wg, wu, wd, keys, vals, qs, os, nk, nv,
    send, recv, loc,
):
    half = nc * W
    sect = lax.axis_index("sect")
    dev = lax.axis_index("dev")
    core = lax.axis_index("cores")
    xlo = lax.rem(dev // NZ, 2)
    x = sect * 2 + xlo
    y = dev // (2 * NZ)
    z = lax.rem(dev, NZ)

    def at(dx=0, dy=0, dz=0, dc=0):
        px = lax.rem(x + dx, NX)
        py = lax.rem(y + dy, NY)
        pz = lax.rem(z + dz, NZ)
        pc = lax.rem(core + dc, 2)
        return (px // 2, (py * 2 + lax.rem(px, 2)) * NZ + pz, pc)

    def push(src, dst, stage, c, to):
        pltpu.make_async_remote_copy(
            src_ref=src, dst_ref=dst, send_sem=send.at[stage, c], recv_sem=recv.at[stage, c],
            device_id=to, device_id_type=MESH,
        ).start()

    loads = [
        pltpu.make_async_copy(a, b, loc.at[i])
        for i, (a, b) in enumerate(
            ((keys_h, keys), (vals_h, vals), (wg_h, wg), (wu_h, wu), (wd_h, wd))
        )
    ]
    for load in loads:
        load.start()

    peers = (
        [at(dz=k) for k in range(1, NZ)]
        + [at(dy=k) for k in range(1, NY)]
        + [at(dx=k) for k in range(1, NX)]
        + [at(dc=1)]
    )
    barrier = pltpu.get_barrier_semaphore()
    for peer in peers:
        pl.semaphore_signal(barrier, inc=1, device_id=peer, device_id_type=MESH)

    row_i = lax.broadcasted_iota(jnp.int32, (R, R), 0)
    col_i = lax.broadcasted_iota(jnp.int32, (R, R), 1)
    same = jnp.where(row_i == col_i, 1.0, 0.0)

    def turned(v):
        return lax.dot_general(
            same, v, (((1,), (1,)), ((), ())),
            precision=lax.Precision.HIGHEST, preferred_element_type=F32,
        )

    routes = turned(routes_t[...].astype(F32))
    gates = turned(gates_t[...])
    lane = lax.broadcasted_iota(jnp.int32, (R, 128), 1)
    lane_f = lane.astype(F32)
    named = jnp.zeros((R, 128), F32)
    weight = jnp.zeros((R, 128), F32)
    for k in range(routes.shape[1]):
        route = routes[:, k : k + 1]
        named = named + jnp.where(lane_f == route, 1.0, 0.0)
        weight = weight + jnp.where(lane_f == route + 64.0, gates[:, k : k + 1], 0.0)
    earlier = dot(jnp.where(col_i < row_i, 1.0, 0.0).astype(BF16), named.astype(BF16))
    cb[0, :R] = jnp.where(lane < 64, jnp.where(named > 0.5, earlier, -1.0), weight)

    def own_rows(c):
        cols = pl.ds(pl.multiple_of(core * half + c * W, W), W)
        return hid[:, cols].astype(F32)

    def stage_rows(c, _):
        hs[c] = jnp.concatenate([own_rows(c), jnp.zeros((RP - R, W), F32)], axis=0).astype(BF16)
        return 0

    lax.fori_loop(0, nc, stage_rows, 0)

    pl.semaphore_wait(barrier, len(peers))

    def send_rows(c, _):
        push(hs.at[c], hp.at[c], 0, c, at(dx=2))
        return 0

    push(hs.at[0], hp.at[0], 0, 0, at(dx=2))
    push(cb.at[0, pl.ds(0, R)], cb.at[0, pl.ds(R, R)], 7, 0, at(dx=2))
    lax.fori_loop(1, nc, send_rows, 0)

    nk[...] = new_k[...].astype(F32)
    nv[...] = new_v[...].astype(F32)
    heads = query.shape[1] // HD
    for h in range(heads):
        qs[:, h, :] = query[:, h * HD : (h + 1) * HD].astype(F32)
    gacc[...] = jnp.zeros_like(gacc)
    uacc[...] = jnp.zeros_like(uacc)

    wait_bytes(cb.at[0, pl.ds(R, R)], recv.at[7, 0])

    def send_codes():
        for k in (4, 1, 7, 2, 6, 3, 5):
            push(cb.at[0], cb.at[NZ - k], 7, 1, at(dz=k))

    def tables():
        wait_bytes(cb.at[pl.ds(1, NZ - 1)], recv.at[7, 1])
        ct[...] = cb[...].reshape(ZR, 128).T
        slot_i = lax.broadcasted_iota(jnp.int32, (S, ZR), 0)
        slot_b = slot_i // CAP
        slot_s = (slot_i - slot_b * CAP).astype(F32)
        place = lax.broadcasted_iota(jnp.int32, (S, ZR), 1)
        place_b = place // (2 * R)
        partner = place - place_b * (2 * R) >= R
        here = slot_b == place_b
        for d in range(NY):
            for kind in range(3):
                q = kind // 2
                expert = (lax.rem(y + d, NY) * 2 + lax.rem(xlo + q, 2)) * NZ + z
                block = partner if kind == 1 else jnp.logical_not(partner)
                mask = here & block & (ct[pl.ds(expert, 1), :] == slot_s)
                at_row = (d * 3 + kind) * S
                pick[at_row : at_row + S, :] = jnp.where(mask, 1.0, 0.0).astype(BF16)
                wtab[at_row : at_row + S, :] = jnp.where(mask, ct[pl.ds(expert + 64, 1), :], 0.0)

    scale = HD ** (-0.5)

    def attend(r):
        length = lens[r]
        q = qs[r]
        q0, q1 = q[: heads // 2], q[heads // 2 :]
        empty = jnp.zeros_like(q0)
        wide = jnp.concatenate(
            [jnp.concatenate([q0, empty], axis=1), jnp.concatenate([empty, q1], axis=1)], axis=0
        ).astype(BF16)
        scores = dot_nt(wide, keys[r]) * scale
        valid = lax.broadcasted_iota(jnp.int32, scores.shape, 1) < length
        scores = jnp.where(valid, scores, -jnp.inf)
        fresh_k = nk[pl.ds(r, 1), :]
        fresh_v = nv[pl.ds(r, 1), :]
        own = jnp.concatenate(
            [
                jnp.sum(q0 * fresh_k[:, :HD], axis=1, keepdims=True),
                jnp.sum(q1 * fresh_k[:, HD:], axis=1, keepdims=True),
            ],
            axis=0,
        ) * scale
        top = jnp.maximum(jnp.max(scores, axis=1, keepdims=True), own)
        probs = jnp.exp(scores - top)
        own_p = jnp.exp(own - top)
        total = jnp.sum(probs, axis=1, keepdims=True) + own_p
        probs_b = (probs / total).astype(BF16)
        own_b = (own_p / total).astype(BF16).astype(F32)
        mixed = dot(probs_b, vals[r])
        n = heads // 2
        os[r, :n] = mixed[:n, :HD] + own_b[:n] * fresh_v[:, :HD]
        os[r, n:] = mixed[n:, HD:] + own_b[n:] * fresh_v[:, HD:]

    per_step = -(-R // nc)
    half_rows = NX * NY * S // 2

    def gate_up(x_ref, c, base):
        depth = pl.ds(pl.multiple_of(base + c * W, W), W)

        def part(i, _):
            rows = pl.ds(pl.multiple_of(i * half_rows, half_rows), half_rows)
            block = x_ref[c, pl.ds(i * 2, 2)].reshape(half_rows, W)
            gacc[rows, :] += dot(block, wg[depth, :])
            uacc[rows, :] += dot(block, wu[depth, :])
            return 0

        lax.fori_loop(0, 2, part, 0)

    def forward(t, _):
        @pl.when(t < nc)
        def _():
            c = t
            wait_bytes(hp.at[c], recv.at[0, c])
            zb[c, 0] = jnp.concatenate([own_rows(c), hp[c].astype(F32)[:R]], axis=0).astype(BF16)
            push(zb.at[c, 0], zb.at[c, 4], 1, c, at(dz=4))
            push(zb.at[c, 0], zb.at[c, 7], 1, c, at(dz=1))
            push(zb.at[c, 0], zb.at[c, 1], 1, c, at(dz=7))

        @pl.when(t == 0)
        def _():
            send_codes()

        @pl.when((t >= F_LAGS[0]) & (t < nc + F_LAGS[0]))
        def _():
            c = t - F_LAGS[0]
            wait_bytes(zb.at[c, pl.ds(1, 3)], recv.at[1, c])
            push(zb.at[c, 4], zb.at[c, 3], 2, c, at(dz=1))
            push(zb.at[c, 4], zb.at[c, 5], 2, c, at(dz=7))
            push(zb.at[c, 7], zb.at[c, 6], 2, c, at(dz=1))
            push(zb.at[c, 1], zb.at[c, 2], 2, c, at(dz=7))

        @pl.when(t == F_LAGS[1])
        def _():
            tables()

        @pl.when((t >= F_LAGS[1]) & (t < nc + F_LAGS[1]))
        def _():
            c = t - F_LAGS[1]
            wait_bytes(zb.at[c, pl.ds(1, 4)], recv.at[2, c])
            chosen = dot(pick[...], zb[c].reshape(ZR, W)).astype(BF16)
            chosen = chosen.reshape(NY, 3, S, W)
            for d in (2, 1, 3):
                ps[c, d - 1] = chosen[d]
                push(ps.at[c, d - 1, 2], ob.at[c, NY - d], 4, c, at(dy=d))
            for d in (2, 1, 3):
                push(ps.at[c, d - 1, pl.ds(0, 2)], xf.at[c, pl.ds(0, 2), NY - d], 3, c, at(dy=d))
            xf[c, 0, 0] = chosen[0, 0]
            xf[c, 1, 0] = chosen[0, 1]
            ob[c, 0] = chosen[0, 2]

        @pl.when((t >= F_LAGS[2]) & (t < nc + F_LAGS[2]))
        def _():
            c = t - F_LAGS[2]
            wait_bytes(ob.at[c, pl.ds(1, NY - 1)], recv.at[4, c])
            push(ob.at[c], xf.at[c, 3], 5, c, at(dx=1))
            push(ob.at[c], xf.at[c, 2], 5, c, at(dx=3))

        @pl.when((t >= F_LAGS[3]) & (t < nc + F_LAGS[3]))
        def _():
            c = t - F_LAGS[3]
            wait_bytes(xf.at[c, pl.ds(0, 2), pl.ds(1, NY - 1)], recv.at[3, c])
            wait_bytes(xf.at[c, pl.ds(2, 2)], recv.at[5, c])
            push(xf.at[c], xo.at[c], 6, c, at(dc=1))
            gate_up(xf, c, core * half)

        @pl.when((t >= F_LAGS[4]) & (t < nc + F_LAGS[4]))
        def _():
            c = t - F_LAGS[4]
            wait_bytes(xo.at[c], recv.at[6, c])
            gate_up(xo, c, (1 - core) * half)

        @pl.when(t == 0)
        def _():
            loads[0].wait()
            loads[1].wait()

        @pl.when(t * per_step < R)
        def _():
            for i in range(per_step):
                attend(t * per_step + i)

        @pl.when(t == 1)
        def _():
            loads[2].wait()
            loads[3].wait()

        @pl.when(t == nc)
        def _():
            weights = wtab[...].T
            high = weights.astype(BF16)
            whl[0] = high
            whl[1] = (weights - high.astype(F32)).astype(BF16)

        return 0

    lax.fori_loop(0, nc + F_LAGS[-1], forward, 0)

    def activate(i, _):
        rows = pl.ds(pl.multiple_of(i * S, S), S)
        gate = gacc[rows, :]
        act[rows, :] = (gate * jax.nn.sigmoid(gate) * uacc[rows, :]).astype(BF16)
        return 0

    lax.fori_loop(0, NX * NY, activate, 0)
    loads[4].wait()

    def down(c, base, i):
        depth = pl.ds(pl.multiple_of(base + c * W, W), W)
        rows = pl.ds(pl.multiple_of(i * half_rows, half_rows), half_rows)
        return dot_nt(act[rows, :], wd[depth, :])

    def plus(a, *others):
        total = a.astype(F32)
        for b in others:
            total = total + b.astype(F32)
        return total

    def backward(t, _):
        @pl.when(t < nc)
        def _():
            c = t

            def part(i, _):
                got = down(c, (1 - core) * half, i)
                so[c, pl.ds(i * 2, 2)] = got.astype(BF16).reshape(2, NY, S, W)
                return 0

            lax.fori_loop(0, 2, part, 0)
            push(so.at[c], ro.at[c], 8, c, at(dc=1))

        @pl.when((t >= B_LAGS[0]) & (t < nc + B_LAGS[0]))
        def _():
            c = t - B_LAGS[0]
            wait_bytes(ro.at[c], recv.at[8, c])

            def part(i, _):
                theirs = ro[c, pl.ds(i * 2, 2)].reshape(half_rows, W)
                got = down(c, core * half, i) + theirs.astype(F32)
                sx[c, pl.ds(i * 2, 2)] = got.astype(BF16).reshape(2, NY, S, W)
                return 0

            lax.fori_loop(0, 2, part, 0)
            push(sx.at[c, 2], rx.at[c, 0], 9, c, at(dx=1))
            push(sx.at[c, 3], rx.at[c, 1], 9, c, at(dx=3))
            for j in (2, 1, 3):
                push(sx.at[c, pl.ds(0, 2), j], ry.at[c, NY - j, pl.ds(0, 2)], 10, c, at(dy=j))
            ry[c, 0, 0] = sx[c, 0, 0]
            ry[c, 0, 1] = sx[c, 1, 0]

        @pl.when((t >= B_LAGS[1]) & (t < nc + B_LAGS[1]))
        def _():
            c = t - B_LAGS[1]
            wait_bytes(rx.at[c], recv.at[9, c])
            for j in (2, 1, 3):
                sy[c, j - 1] = plus(rx[c, 0, j], rx[c, 1, j]).astype(BF16)
                push(sy.at[c, j - 1], ry.at[c, NY - j, 2], 11, c, at(dy=j))
            ry[c, 0, 2] = plus(rx[c, 0, 0], rx[c, 1, 0]).astype(BF16)

        @pl.when((t >= B_LAGS[2]) & (t < nc + B_LAGS[2]))
        def _():
            c = t - B_LAGS[2]
            wait_bytes(ry.at[c, pl.ds(1, NY - 1), pl.ds(0, 2)], recv.at[10, c])
            wait_bytes(ry.at[c, pl.ds(1, NY - 1), 2], recv.at[11, c])
            slots = ry[c].reshape(NY * 3 * S, W)
            sums = dot(whl[0], slots) + dot(whl[1], slots)
            sz[c] = sums.astype(BF16).reshape(NZ, 2 * R, W)
            push(sz.at[c, 6], r1.at[c, 0], 12, c, at(dz=7))
            push(sz.at[c, 2], r1.at[c, 1], 12, c, at(dz=1))
            push(sz.at[c, 5], r1.at[c, 2], 12, c, at(dz=1))
            push(sz.at[c, 3], r1.at[c, 3], 12, c, at(dz=7))

        @pl.when((t >= B_LAGS[3]) & (t < nc + B_LAGS[3]))
        def _():
            c = t - B_LAGS[3]
            wait_bytes(r1.at[c], recv.at[12, c])
            s2[c, 2] = plus(sz[c, 4], r1[c, 2], r1[c, 3]).astype(BF16)
            push(s2.at[c, 2], r2.at[c, 2], 13, c, at(dz=4))
            s2[c, 0] = plus(sz[c, 7], r1[c, 0]).astype(BF16)
            push(s2.at[c, 0], r2.at[c, 0], 13, c, at(dz=7))
            s2[c, 1] = plus(sz[c, 1], r1[c, 1]).astype(BF16)
            push(s2.at[c, 1], r2.at[c, 1], 13, c, at(dz=1))

        @pl.when((t >= B_LAGS[4]) & (t < nc + B_LAGS[4]))
        def _():
            c = t - B_LAGS[4]
            wait_bytes(r2.at[c], recv.at[13, c])
            total = plus(sz[c, 0], r2[c, 0], r2[c, 1], r2[c, 2])
            fo[c] = total[:R]
            fs[c] = jnp.concatenate([total[R:], jnp.zeros((RP - R, W), F32)], axis=0).astype(BF16)
            push(fs.at[c], fr.at[c], 14, c, at(dx=2))

        @pl.when((t >= B_LAGS[5]) & (t < nc + B_LAGS[5]))
        def _():
            c = t - B_LAGS[5]
            wait_bytes(fr.at[c], recv.at[14, c])
            cols = pl.ds(pl.multiple_of(c * W, W), W)
            out[:, cols] = (fo[c] + fr[c].astype(F32)[:R]).astype(BF16)

        @pl.when(t == 2)
        def _():
            for h in range(heads):
                att_out[:, h * HD : (h + 1) * HD] = os[:, h, :].astype(BF16)

        return 0

    lax.fori_loop(0, nc + B_LAGS[-1], backward, 0)

    def drain(c, _):
        wait_bytes(hp.at[c], send.at[0, c])
        wait_bytes(zb.at[c, pl.ds(1, 3)], send.at[1, c])
        wait_bytes(zb.at[c, pl.ds(1, 4)], send.at[2, c])
        wait_bytes(xf.at[c, pl.ds(0, 2), pl.ds(1, NY - 1)], send.at[3, c])
        wait_bytes(ob.at[c, pl.ds(1, NY - 1)], send.at[4, c])
        wait_bytes(xf.at[c, pl.ds(2, 2)], send.at[5, c])
        wait_bytes(xo.at[c], send.at[6, c])
        wait_bytes(ro.at[c], send.at[8, c])
        wait_bytes(rx.at[c], send.at[9, c])
        wait_bytes(ry.at[c, pl.ds(1, NY - 1), pl.ds(0, 2)], send.at[10, c])
        wait_bytes(ry.at[c, pl.ds(1, NY - 1), 2], send.at[11, c])
        wait_bytes(r1.at[c], send.at[12, c])
        wait_bytes(r2.at[c], send.at[13, c])
        wait_bytes(fr.at[c], send.at[14, c])
        return 0

    wait_bytes(cb.at[0, pl.ds(R, R)], send.at[7, 0])
    wait_bytes(cb.at[pl.ds(1, NZ - 1)], send.at[7, 1])
    lax.fori_loop(0, nc, drain, 0)


def per_device(
    query, cache_keys, cache_values, new_key, new_value, lengths,
    hidden, routes, gate_weights, w_gate, w_up, w_down,
):
    width = hidden.shape[1]
    nc = width // 2 // W
    inner = w_gate.shape[2]
    rows = NX * NY * S
    heads = query.shape[1] // HD
    vmem = pl.BlockSpec(memory_space=pltpu.VMEM)
    smem = pl.BlockSpec(memory_space=pltpu.SMEM)
    hbm = pl.BlockSpec(memory_space=pl.ANY)
    shapes = [
        ((nc, RP, W), BF16),
        ((nc, RP, W), BF16),
        ((nc, NZ, 2 * R, W), BF16),
        ((NZ, 2 * R, 128), F32),
        ((128, ZR), F32),
        ((NY * 3 * S, ZR), BF16),
        ((NY * 3 * S, ZR), F32),
        ((2, ZR, NY * 3 * S), BF16),
        ((nc, NY - 1, 3, S, W), BF16),
        ((nc, NY, S, W), BF16),
        ((nc, NX, NY, S, W), BF16),
        ((nc, NX, NY, S, W), BF16),
        ((rows, inner), F32),
        ((rows, inner), F32),
        ((rows, inner), BF16),
        ((nc, NX, NY, S, W), BF16),
        ((nc, NX, NY, S, W), BF16),
        ((nc, NX, NY, S, W), BF16),
        ((nc, 2, NY, S, W), BF16),
        ((nc, NY - 1, S, W), BF16),
        ((nc, NY, 3, S, W), BF16),
        ((nc, NZ, 2 * R, W), BF16),
        ((nc, 4, 2 * R, W), BF16),
        ((nc, 3, 2 * R, W), BF16),
        ((nc, 3, 2 * R, W), BF16),
        ((nc, R, W), F32),
        ((nc, RP, W), BF16),
        ((nc, RP, W), BF16),
        ((width, inner), BF16),
        ((width, inner), BF16),
        ((width, inner), BF16),
        (cache_keys.shape, BF16),
        (cache_values.shape, BF16),
        ((R, heads, HD), F32),
        ((R, heads, HD), F32),
        (new_key.shape, F32),
        (new_value.shape, F32),
    ]
    return pl.pallas_call(
        functools.partial(body, nc),
        out_shape=(pltpu.VMEM(query.shape, BF16), pltpu.VMEM((R, width // 2), BF16)),
        in_specs=[vmem, vmem, vmem, smem, vmem, vmem, vmem, hbm, hbm, hbm, hbm, hbm],
        out_specs=(vmem, vmem),
        scratch_shapes=[pltpu.VMEM(s, t) for s, t in shapes]
        + [
            pltpu.SemaphoreType.DMA((15, nc)),
            pltpu.SemaphoreType.DMA((15, nc)),
            pltpu.SemaphoreType.DMA((5,)),
        ],
        compiler_params=pltpu.CompilerParams(
            collective_id=0, has_side_effects=True, vmem_limit_bytes=60 * 1024 * 1024
        ),
        name="experts",
    )(
        hidden, routes.T, gate_weights.T, lengths, query, new_key, new_value,
        cache_keys, cache_values, w_gate[0], w_up[0], w_down[0],
    )


def solution(mesh):
    rows = ("sect", "dev")
    cols = ("sect", "cores")
    in_specs = (
        P(rows, "cores"),
        P(rows, None, "cores"),
        P(rows, None, "cores"),
        P(rows, "cores"),
        P(rows, "cores"),
        P(rows),
        P(rows, None),
        P(rows, None),
        P(rows, None),
        P("dev", None, cols),
        P("dev", None, cols),
        P("dev", None, cols),
    )
    out_specs = (P(rows, "cores"), P(rows, "cores"))
    return jax.shard_map(
        per_device, mesh=mesh, in_specs=in_specs, out_specs=out_specs, check_vma=False
    )
```

```python
import functools

import jax
import jax.numpy as jnp
from jax import lax
from jax.experimental import pallas as pl
from jax.experimental.pallas import tpu as pltpu
from jax.sharding import PartitionSpec as P

MESH = pl.DeviceIdType.MESH
HD = 128
NX, NY, NZ = 4, 4, 8
R = 24
RP = 32
CAP = 6
ZR = NZ * 2 * R
S = NZ * CAP
W = 256
F_LAGS = (2, 4, 6, 8, 9)
B_LAGS = (1, 2, 4, 6, 8, 10)
F32 = jnp.float32
BF16 = jnp.bfloat16


def dot(a, b):
    return jnp.dot(a, b, preferred_element_type=F32)


def dot_nt(a, b):
    return lax.dot_general(a, b, (((1,), (1,)), ((), ())), preferred_element_type=F32)


def wait_bytes(ref, sem):
    pltpu.make_async_copy(ref, ref, sem).wait()


def body(
    nc,
    hid, routes_t, gates_t, lens, query, new_k, new_v, keys_h, vals_h, wg_h, wu_h, wd_h,
    att_out, out,
    hs, hp, zb, cb, ct, pick, wtab, whl, ps, ob, xf, xo, gacc, uacc, act,
    so, ro, sx, rx, sy, ry, sz, r1, s2, r2, fo, fs, fr, wg, wu, wd, keys, vals, qs, os, nk, nv,
    send, recv, loc,
):
    half = nc * W
    sect = lax.axis_index("sect")
    dev = lax.axis_index("dev")
    core = lax.axis_index("cores")
    xlo = lax.rem(dev // NZ, 2)
    x = sect * 2 + xlo
    y = dev // (2 * NZ)
    z = lax.rem(dev, NZ)

    def at(dx=0, dy=0, dz=0, dc=0):
        px = lax.rem(x + dx, NX)
        py = lax.rem(y + dy, NY)
        pz = lax.rem(z + dz, NZ)
        pc = lax.rem(core + dc, 2)
        return (px // 2, (py * 2 + lax.rem(px, 2)) * NZ + pz, pc)

    def push(src, dst, stage, c, to):
        pltpu.make_async_remote_copy(
            src_ref=src, dst_ref=dst, send_sem=send.at[stage, c], recv_sem=recv.at[stage, c],
            device_id=to, device_id_type=MESH,
        ).start()

    loads = [
        pltpu.make_async_copy(a, b, loc.at[i])
        for i, (a, b) in enumerate(
            ((keys_h, keys), (vals_h, vals), (wg_h, wg), (wu_h, wu), (wd_h, wd))
        )
    ]
    for load in loads:
        load.start()

    peers = (
        [at(dz=k) for k in range(1, NZ)]
        + [at(dy=k) for k in range(1, NY)]
        + [at(dx=k) for k in range(1, NX)]
        + [at(dc=1)]
    )
    barrier = pltpu.get_barrier_semaphore()
    for peer in peers:
        pl.semaphore_signal(barrier, inc=1, device_id=peer, device_id_type=MESH)

    row_i = lax.broadcasted_iota(jnp.int32, (R, R), 0)
    col_i = lax.broadcasted_iota(jnp.int32, (R, R), 1)
    same = jnp.where(row_i == col_i, 1.0, 0.0)

    def turned(v):
        return lax.dot_general(
            same, v, (((1,), (1,)), ((), ())),
            precision=lax.Precision.HIGHEST, preferred_element_type=F32,
        )

    routes = turned(routes_t[...].astype(F32))
    gates = turned(gates_t[...])
    lane = lax.broadcasted_iota(jnp.int32, (R, 128), 1)
    lane_f = lane.astype(F32)
    named = jnp.zeros((R, 128), F32)
    weight = jnp.zeros((R, 128), F32)
    for k in range(routes.shape[1]):
        route = routes[:, k : k + 1]
        named = named + jnp.where(lane_f == route, 1.0, 0.0)
        weight = weight + jnp.where(lane_f == route + 64.0, gates[:, k : k + 1], 0.0)
    earlier = dot(jnp.where(col_i < row_i, 1.0, 0.0).astype(BF16), named.astype(BF16))
    cb[0, :R] = jnp.where(lane < 64, jnp.where(named > 0.5, earlier, -1.0), weight)

    def own_rows(c):
        cols = pl.ds(pl.multiple_of(core * half + c * W, W), W)
        return hid[:, cols].astype(F32)

    def stage_rows(c, _):
        hs[c] = jnp.concatenate([own_rows(c), jnp.zeros((RP - R, W), F32)], axis=0).astype(BF16)
        return 0

    lax.fori_loop(0, nc, stage_rows, 0)

    pl.semaphore_wait(barrier, len(peers))

    def send_rows(c, _):
        push(hs.at[c], hp.at[c], 0, c, at(dx=2))
        return 0

    push(hs.at[0], hp.at[0], 0, 0, at(dx=2))
    push(cb.at[0, pl.ds(0, R)], cb.at[0, pl.ds(R, R)], 7, 0, at(dx=2))
    lax.fori_loop(1, nc, send_rows, 0)

    nk[...] = new_k[...].astype(F32)
    nv[...] = new_v[...].astype(F32)
    heads = query.shape[1] // HD
    for h in range(heads):
        qs[:, h, :] = query[:, h * HD : (h + 1) * HD].astype(F32)
    gacc[...] = jnp.zeros_like(gacc)
    uacc[...] = jnp.zeros_like(uacc)

    wait_bytes(cb.at[0, pl.ds(R, R)], recv.at[7, 0])

    def send_codes():
        for k in (4, 1, 7, 2, 6, 3, 5):
            push(cb.at[0], cb.at[NZ - k], 7, 1, at(dz=k))

    def tables():
        wait_bytes(cb.at[pl.ds(1, NZ - 1)], recv.at[7, 1])
        ct[...] = cb[...].reshape(ZR, 128).T
        slot_i = lax.broadcasted_iota(jnp.int32, (S, ZR), 0)
        slot_b = slot_i // CAP
        slot_s = (slot_i - slot_b * CAP).astype(F32)
        place = lax.broadcasted_iota(jnp.int32, (S, ZR), 1)
        place_b = place // (2 * R)
        partner = place - place_b * (2 * R) >= R
        here = slot_b == place_b
        for d in range(NY):
            for kind in range(3):
                q = kind // 2
                expert = (lax.rem(y + d, NY) * 2 + lax.rem(xlo + q, 2)) * NZ + z
                block = partner if kind == 1 else jnp.logical_not(partner)
                mask = here & block & (ct[pl.ds(expert, 1), :] == slot_s)
                at_row = (d * 3 + kind) * S
                pick[at_row : at_row + S, :] = jnp.where(mask, 1.0, 0.0).astype(BF16)
                wtab[at_row : at_row + S, :] = jnp.where(mask, ct[pl.ds(expert + 64, 1), :], 0.0)

    scale = HD ** (-0.5)

    def attend(r):
        length = lens[r]
        q = qs[r]
        q0, q1 = q[: heads // 2], q[heads // 2 :]
        empty = jnp.zeros_like(q0)
        wide = jnp.concatenate(
            [jnp.concatenate([q0, empty], axis=1), jnp.concatenate([empty, q1], axis=1)], axis=0
        ).astype(BF16)
        scores = dot_nt(wide, keys[r]) * scale
        valid = lax.broadcasted_iota(jnp.int32, scores.shape, 1) < length
        scores = jnp.where(valid, scores, -jnp.inf)
        fresh_k = nk[pl.ds(r, 1), :]
        fresh_v = nv[pl.ds(r, 1), :]
        own = jnp.concatenate(
            [
                jnp.sum(q0 * fresh_k[:, :HD], axis=1, keepdims=True),
                jnp.sum(q1 * fresh_k[:, HD:], axis=1, keepdims=True),
            ],
            axis=0,
        ) * scale
        top = jnp.maximum(jnp.max(scores, axis=1, keepdims=True), own)
        probs = jnp.exp(scores - top)
        own_p = jnp.exp(own - top)
        total = jnp.sum(probs, axis=1, keepdims=True) + own_p
        probs_b = (probs / total).astype(BF16)
        own_b = (own_p / total).astype(BF16).astype(F32)
        mixed = dot(probs_b, vals[r])
        n = heads // 2
        os[r, :n] = mixed[:n, :HD] + own_b[:n] * fresh_v[:, :HD]
        os[r, n:] = mixed[n:, HD:] + own_b[n:] * fresh_v[:, HD:]

    per_step = 2
    half_rows = NX * NY * S // 2

    def gate_up(x_ref, c, base):
        depth = pl.ds(pl.multiple_of(base + c * W, W), W)

        def part(i, _):
            rows = pl.ds(pl.multiple_of(i * half_rows, half_rows), half_rows)
            block = x_ref[c, pl.ds(i * 2, 2)].reshape(half_rows, W)
            gacc[rows, :] += dot(block, wg[depth, :])
            uacc[rows, :] += dot(block, wu[depth, :])
            return 0

        lax.fori_loop(0, 2, part, 0)

    def forward(t, _):
        @pl.when(t < nc)
        def _():
            c = t
            wait_bytes(hp.at[c], recv.at[0, c])
            zb[c, 0] = jnp.concatenate([own_rows(c), hp[c].astype(F32)[:R]], axis=0).astype(BF16)
            push(zb.at[c, 0], zb.at[c, 4], 1, c, at(dz=4))
            push(zb.at[c, 0], zb.at[c, 7], 1, c, at(dz=1))
            push(zb.at[c, 0], zb.at[c, 1], 1, c, at(dz=7))

        @pl.when(t == 0)
        def _():
            send_codes()

        @pl.when((t >= F_LAGS[0]) & (t < nc + F_LAGS[0]))
        def _():
            c = t - F_LAGS[0]
            wait_bytes(zb.at[c, pl.ds(1, 3)], recv.at[1, c])
            push(zb.at[c, 4], zb.at[c, 3], 2, c, at(dz=1))
            push(zb.at[c, 4], zb.at[c, 5], 2, c, at(dz=7))
            push(zb.at[c, 7], zb.at[c, 6], 2, c, at(dz=1))
            push(zb.at[c, 1], zb.at[c, 2], 2, c, at(dz=7))

        @pl.when(t == F_LAGS[1])
        def _():
            tables()

        @pl.when((t >= F_LAGS[1]) & (t < nc + F_LAGS[1]))
        def _():
            c = t - F_LAGS[1]
            wait_bytes(zb.at[c, pl.ds(1, 4)], recv.at[2, c])
            chosen = dot(pick[...], zb[c].reshape(ZR, W)).astype(BF16)
            chosen = chosen.reshape(NY, 3, S, W)
            for d in (2, 1, 3):
                ps[c, d - 1] = chosen[d]
                push(ps.at[c, d - 1, 2], ob.at[c, NY - d], 4, c, at(dy=d))
            for d in (2, 1, 3):
                push(ps.at[c, d - 1, pl.ds(0, 2)], xf.at[c, pl.ds(0, 2), NY - d], 3, c, at(dy=d))
            xf[c, 0, 0] = chosen[0, 0]
            xf[c, 1, 0] = chosen[0, 1]
            ob[c, 0] = chosen[0, 2]

        @pl.when((t >= F_LAGS[2]) & (t < nc + F_LAGS[2]))
        def _():
            c = t - F_LAGS[2]
            wait_bytes(ob.at[c, pl.ds(1, NY - 1)], recv.at[4, c])
            push(ob.at[c], xf.at[c, 3], 5, c, at(dx=1))
            push(ob.at[c], xf.at[c, 2], 5, c, at(dx=3))

        @pl.when((t >= F_LAGS[3]) & (t < nc + F_LAGS[3]))
        def _():
            c = t - F_LAGS[3]
            wait_bytes(xf.at[c, pl.ds(0, 2), pl.ds(1, NY - 1)], recv.at[3, c])
            wait_bytes(xf.at[c, pl.ds(2, 2)], recv.at[5, c])
            push(xf.at[c], xo.at[c], 6, c, at(dc=1))
            gate_up(xf, c, core * half)

        @pl.when((t >= F_LAGS[4]) & (t < nc + F_LAGS[4]))
        def _():
            c = t - F_LAGS[4]
            wait_bytes(xo.at[c], recv.at[6, c])
            gate_up(xo, c, (1 - core) * half)

        @pl.when(t == 0)
        def _():
            loads[0].wait()
            loads[1].wait()

        @pl.when(t * per_step < R)
        def _():
            for i in range(per_step):
                attend(t * per_step + i)

        @pl.when(t == 1)
        def _():
            loads[2].wait()
            loads[3].wait()

        @pl.when(t == nc)
        def _():
            weights = wtab[...].T
            high = weights.astype(BF16)
            whl[0] = high
            whl[1] = (weights - high.astype(F32)).astype(BF16)

        return 0

    lax.fori_loop(0, nc + F_LAGS[-1], forward, 0)

    def activate(i, _):
        rows = pl.ds(pl.multiple_of(i * S, S), S)
        gate = gacc[rows, :]
        act[rows, :] = (gate * jax.nn.sigmoid(gate) * uacc[rows, :]).astype(BF16)
        return 0

    lax.fori_loop(0, NX * NY, activate, 0)
    loads[4].wait()

    def down(c, base, i):
        depth = pl.ds(pl.multiple_of(base + c * W, W), W)
        rows = pl.ds(pl.multiple_of(i * half_rows, half_rows), half_rows)
        return dot_nt(act[rows, :], wd[depth, :])

    def plus(a, *others):
        total = a.astype(F32)
        for b in others:
            total = total + b.astype(F32)
        return total

    def backward(t, _):
        @pl.when(t < nc)
        def _():
            c = t

            def part(i, _):
                got = down(c, (1 - core) * half, i)
                so[c, pl.ds(i * 2, 2)] = got.astype(BF16).reshape(2, NY, S, W)
                return 0

            lax.fori_loop(0, 2, part, 0)
            push(so.at[c], ro.at[c], 8, c, at(dc=1))

        @pl.when((t >= B_LAGS[0]) & (t < nc + B_LAGS[0]))
        def _():
            c = t - B_LAGS[0]
            wait_bytes(ro.at[c], recv.at[8, c])

            def part(i, _):
                theirs = ro[c, pl.ds(i * 2, 2)].reshape(half_rows, W)
                got = down(c, core * half, i) + theirs.astype(F32)
                sx[c, pl.ds(i * 2, 2)] = got.astype(BF16).reshape(2, NY, S, W)
                return 0

            lax.fori_loop(0, 2, part, 0)
            push(sx.at[c, 2], rx.at[c, 0], 9, c, at(dx=1))
            push(sx.at[c, 3], rx.at[c, 1], 9, c, at(dx=3))
            for j in (2, 1, 3):
                push(sx.at[c, pl.ds(0, 2), j], ry.at[c, NY - j, pl.ds(0, 2)], 10, c, at(dy=j))
            ry[c, 0, 0] = sx[c, 0, 0]
            ry[c, 0, 1] = sx[c, 1, 0]

        @pl.when((t >= B_LAGS[1]) & (t < nc + B_LAGS[1]))
        def _():
            c = t - B_LAGS[1]
            wait_bytes(rx.at[c], recv.at[9, c])
            for j in (2, 1, 3):
                sy[c, j - 1] = plus(rx[c, 0, j], rx[c, 1, j]).astype(BF16)
                push(sy.at[c, j - 1], ry.at[c, NY - j, 2], 11, c, at(dy=j))
            ry[c, 0, 2] = plus(rx[c, 0, 0], rx[c, 1, 0]).astype(BF16)

        @pl.when((t >= B_LAGS[2]) & (t < nc + B_LAGS[2]))
        def _():
            c = t - B_LAGS[2]
            wait_bytes(ry.at[c, pl.ds(1, NY - 1), pl.ds(0, 2)], recv.at[10, c])
            wait_bytes(ry.at[c, pl.ds(1, NY - 1), 2], recv.at[11, c])
            slots = ry[c].reshape(NY * 3 * S, W)
            sums = dot(whl[0], slots) + dot(whl[1], slots)
            sz[c] = sums.astype(BF16).reshape(NZ, 2 * R, W)
            push(sz.at[c, 6], r1.at[c, 0], 12, c, at(dz=7))
            push(sz.at[c, 2], r1.at[c, 1], 12, c, at(dz=1))
            push(sz.at[c, 5], r1.at[c, 2], 12, c, at(dz=1))
            push(sz.at[c, 3], r1.at[c, 3], 12, c, at(dz=7))

        @pl.when((t >= B_LAGS[3]) & (t < nc + B_LAGS[3]))
        def _():
            c = t - B_LAGS[3]
            wait_bytes(r1.at[c], recv.at[12, c])
            s2[c, 2] = plus(sz[c, 4], r1[c, 2], r1[c, 3]).astype(BF16)
            push(s2.at[c, 2], r2.at[c, 2], 13, c, at(dz=4))
            s2[c, 0] = plus(sz[c, 7], r1[c, 0]).astype(BF16)
            push(s2.at[c, 0], r2.at[c, 0], 13, c, at(dz=7))
            s2[c, 1] = plus(sz[c, 1], r1[c, 1]).astype(BF16)
            push(s2.at[c, 1], r2.at[c, 1], 13, c, at(dz=1))

        @pl.when((t >= B_LAGS[4]) & (t < nc + B_LAGS[4]))
        def _():
            c = t - B_LAGS[4]
            wait_bytes(r2.at[c], recv.at[13, c])
            total = plus(sz[c, 0], r2[c, 0], r2[c, 1], r2[c, 2])
            fo[c] = total[:R]
            fs[c] = jnp.concatenate([total[R:], jnp.zeros((RP - R, W), F32)], axis=0).astype(BF16)
            push(fs.at[c], fr.at[c], 14, c, at(dx=2))

        @pl.when((t >= B_LAGS[5]) & (t < nc + B_LAGS[5]))
        def _():
            c = t - B_LAGS[5]
            wait_bytes(fr.at[c], recv.at[14, c])
            cols = pl.ds(pl.multiple_of(c * W, W), W)
            out[:, cols] = (fo[c] + fr[c].astype(F32)[:R]).astype(BF16)

        @pl.when(t == 2)
        def _():
            for h in range(heads):
                att_out[:, h * HD : (h + 1) * HD] = os[:, h, :].astype(BF16)

        return 0

    lax.fori_loop(0, nc + B_LAGS[-1], backward, 0)

    def drain(c, _):
        wait_bytes(hp.at[c], send.at[0, c])
        wait_bytes(zb.at[c, pl.ds(1, 3)], send.at[1, c])
        wait_bytes(zb.at[c, pl.ds(1, 4)], send.at[2, c])
        wait_bytes(xf.at[c, pl.ds(0, 2), pl.ds(1, NY - 1)], send.at[3, c])
        wait_bytes(ob.at[c, pl.ds(1, NY - 1)], send.at[4, c])
        wait_bytes(xf.at[c, pl.ds(2, 2)], send.at[5, c])
        wait_bytes(xo.at[c], send.at[6, c])
        wait_bytes(ro.at[c], send.at[8, c])
        wait_bytes(rx.at[c], send.at[9, c])
        wait_bytes(ry.at[c, pl.ds(1, NY - 1), pl.ds(0, 2)], send.at[10, c])
        wait_bytes(ry.at[c, pl.ds(1, NY - 1), 2], send.at[11, c])
        wait_bytes(r1.at[c], send.at[12, c])
        wait_bytes(r2.at[c], send.at[13, c])
        wait_bytes(fr.at[c], send.at[14, c])
        return 0

    wait_bytes(cb.at[0, pl.ds(R, R)], send.at[7, 0])
    wait_bytes(cb.at[pl.ds(1, NZ - 1)], send.at[7, 1])
    lax.fori_loop(0, nc, drain, 0)


def per_device(
    query, cache_keys, cache_values, new_key, new_value, lengths,
    hidden, routes, gate_weights, w_gate, w_up, w_down,
):
    width = hidden.shape[1]
    nc = width // 2 // W
    inner = w_gate.shape[2]
    rows = NX * NY * S
    heads = query.shape[1] // HD
    vmem = pl.BlockSpec(memory_space=pltpu.VMEM)
    smem = pl.BlockSpec(memory_space=pltpu.SMEM)
    hbm = pl.BlockSpec(memory_space=pl.ANY)
    shapes = [
        ((nc, RP, W), BF16),
        ((nc, RP, W), BF16),
        ((nc, NZ, 2 * R, W), BF16),
        ((NZ, 2 * R, 128), F32),
        ((128, ZR), F32),
        ((NY * 3 * S, ZR), BF16),
        ((NY * 3 * S, ZR), F32),
        ((2, ZR, NY * 3 * S), BF16),
        ((nc, NY - 1, 3, S, W), BF16),
        ((nc, NY, S, W), BF16),
        ((nc, NX, NY, S, W), BF16),
        ((nc, NX, NY, S, W), BF16),
        ((rows, inner), F32),
        ((rows, inner), F32),
        ((rows, inner), BF16),
        ((nc, NX, NY, S, W), BF16),
        ((nc, NX, NY, S, W), BF16),
        ((nc, NX, NY, S, W), BF16),
        ((nc, 2, NY, S, W), BF16),
        ((nc, NY - 1, S, W), BF16),
        ((nc, NY, 3, S, W), BF16),
        ((nc, NZ, 2 * R, W), BF16),
        ((nc, 4, 2 * R, W), BF16),
        ((nc, 3, 2 * R, W), BF16),
        ((nc, 3, 2 * R, W), BF16),
        ((nc, R, W), F32),
        ((nc, RP, W), BF16),
        ((nc, RP, W), BF16),
        ((width, inner), BF16),
        ((width, inner), BF16),
        ((width, inner), BF16),
        (cache_keys.shape, BF16),
        (cache_values.shape, BF16),
        ((R, heads, HD), F32),
        ((R, heads, HD), F32),
        (new_key.shape, F32),
        (new_value.shape, F32),
    ]
    return pl.pallas_call(
        functools.partial(body, nc),
        out_shape=(pltpu.VMEM(query.shape, BF16), pltpu.VMEM((R, width // 2), BF16)),
        in_specs=[vmem, vmem, vmem, smem, vmem, vmem, vmem, hbm, hbm, hbm, hbm, hbm],
        out_specs=(vmem, vmem),
        scratch_shapes=[pltpu.VMEM(s, t) for s, t in shapes]
        + [
            pltpu.SemaphoreType.DMA((15, nc)),
            pltpu.SemaphoreType.DMA((15, nc)),
            pltpu.SemaphoreType.DMA((5,)),
        ],
        compiler_params=pltpu.CompilerParams(
            collective_id=0, has_side_effects=True, vmem_limit_bytes=60 * 1024 * 1024
        ),
        name="experts",
    )(
        hidden, routes.T, gate_weights.T, lengths, query, new_key, new_value,
        cache_keys, cache_values, w_gate[0], w_up[0], w_down[0],
    )


def solution(mesh):
    rows = ("sect", "dev")
    cols = ("sect", "cores")
    in_specs = (
        P(rows, "cores"),
        P(rows, None, "cores"),
        P(rows, None, "cores"),
        P(rows, "cores"),
        P(rows, "cores"),
        P(rows),
        P(rows, None),
        P(rows, None),
        P(rows, None),
        P("dev", None, cols),
        P("dev", None, cols),
        P("dev", None, cols),
    )
    out_specs = (P(rows, "cores"), P(rows, "cores"))
    return jax.shard_map(
        per_device, mesh=mesh, in_specs=in_specs, out_specs=out_specs, check_vma=False
    )
```
